32 devices in a mesh: seq: 8 (over y, x, core), tp: 4 (over z).
Axes of the slice: x: 2, y: 2, z: 4, core: 2. Of those that a mesh axis runs over, the one named last changes fastest.
Arguments:
- query_rows: bfloat16 [1024, 4096], P('seq', 'tp'), may hold values from -6 to 6
- key_rows: bfloat16 [1024, 4096], P('seq', 'tp'), may hold values from -6 to 6
- value_rows: bfloat16 [1024, 4096], P('seq', 'tp'), may hold values from -6 to 6
- short_taps: float32 [3, 4096], P(None, 'tp'), may hold values from -3.5 to 3.5
- decay_rates: float32 [256, 16], P('tp'), may hold values from 0 to 1, as said below
- residues: float32 [256, 16], P('tp'), may hold values from -1 to 1
- skip_gain: float32 [4096], P('tp'), may hold values from -4 to 4
- out_weight: bfloat16 [4096, 4096], P('tp'), may hold values from -0.09375 to 0.09375
Outputs:
- mixed_out: bfloat16 [1024, 4096], P('seq', 'tp')
The draws below stay inside these ranges and needn't reach their ends.
Inputs may be any that keep to these rules, and one draw needn't show every extreme that they name: `decay_rates`: positive decay rates.
All inputs are finite; a program needn't handle non-finite values.
Results may differ from the reference program's by a relative error of at most 0.0095.
Values may be sent and summed in bfloat16 or wider, within the bound.
A program may use at most 64 MiB of HBM per device.

```python
import math
import jax
import jax.numpy as jnp
from jax import lax

CH = 4096
DOUT = 4096
MODES = 16
SEQLEN = 1024
GROUPS = 256
N_TP = 4


def modal_draw(key):
    base_key = jax.random.fold_in(key, 7)
    rate_key, residue_key = jax.random.split(base_key, 2)
    table_shape = (GROUPS, MODES)
    log_low = math.log(0.5 / SEQLEN)
    log_high = math.log(0.5)
    uniform_draw = jax.random.uniform(rate_key, table_shape, jnp.float32)
    rate_values = jnp.exp(log_low + (log_high - log_low) * uniform_draw)
    residue_values = jax.random.normal(residue_key, table_shape, jnp.float32) * jnp.sqrt(2.0 * rate_values / MODES)
    residue_values = jnp.clip(residue_values, -1.0, 1.0)
    return (rate_values.astype(jnp.float32), residue_values.astype(jnp.float32))


def draw_decay_rates(key, part):
    return modal_draw(key)[0]


def draw_residues(key, part):
    return modal_draw(key)[1]


def block_levels(own_key, shape, cuts, low, high):
    level, own = 1.0, jax.random.fold_in(own_key, 6)
    for dim, parts in cuts:
        steps = jnp.exp(jax.random.uniform(jax.random.fold_in(own, dim), (parts,), jnp.float32, low / len(cuts), high / len(cuts)))
        level = level * jnp.repeat(steps, shape[dim] // parts).reshape([-1 if axis == dim else 1 for axis in range(len(shape))])
    return level


def normal_values(rng, extent, deviation, most, shards=(), held_as=jnp.bfloat16):
    drawn = deviation * jax.random.normal(rng, extent, jnp.float32)
    if shards:
        drawn = drawn * block_levels(rng, extent, shards, -0.22, 0.18)
    return jnp.clip(drawn, -most, most).astype(held_as)


def setup_inputs(seed: int = 0) -> dict:
    key_list = jax.random.split(jax.random.key(seed), 9)
    query_rows = normal_values(key_list[0], (SEQLEN, CH), 1.0, 6.0, ((0, 8), (1, 4)))
    key_rows = normal_values(key_list[1], (SEQLEN, CH), 1.0, 6.0, ((0, 8), (1, 4)))
    value_rows = normal_values(key_list[2], (SEQLEN, CH), 1.0, 6.0, ((0, 8), (1, 4)))
    short_taps = normal_values(key_list[3], (3, CH), 3 ** -0.5, 3.5, ((1, 4),), jnp.float32)
    decay_rates = draw_decay_rates(jax.random.fold_in(key_list[8], 71), 0)
    residues = draw_residues(jax.random.fold_in(key_list[8], 71), 0)
    skip_gain = normal_values(key_list[6], (CH,), 1.0, 4.0, ((0, 4),), jnp.float32)
    out_weight = normal_values(key_list[7], (CH, DOUT), CH ** -0.5, 0.09375, ((0, 4),))
    return {"query_rows": query_rows, "key_rows": key_rows, "value_rows": value_rows, "short_taps": short_taps, "decay_rates": decay_rates, "residues": residues, "skip_gain": skip_gain, "out_weight": out_weight}


def featurize(row_block, tap_rows):
    padded = jnp.pad(row_block.astype(jnp.float32), ((2, 0), (0, 0)))
    length_rows = row_block.shape[0]
    return tap_rows[0] * padded[2:] + tap_rows[1] * padded[1:length_rows + 1] + tap_rows[2] * padded[:length_rows]


def reference(query_rows, key_rows, value_rows, short_taps, decay_rates, residues, skip_gain, out_weight):
    query_feat = featurize(query_rows, short_taps)
    key_feat = featurize(key_rows, short_taps)
    value_feat = featurize(value_rows, short_taps)
    source = key_feat * value_feat
    seq_total = source.shape[0]
    group_count = decay_rates.shape[0]
    group_size = source.shape[1] // group_count
    row_steps = jnp.arange(seq_total).astype(jnp.float32)

    def one_group(inputs):
        rate_values, residue_values, group_rows = inputs
        filter_taps = jnp.sum(residue_values[None, :] * jnp.exp(-rate_values[None, :] * row_steps[:, None]), axis=1)
        filter_spec = jnp.fft.fft(jnp.pad(filter_taps, (0, seq_total)))
        padded_spec = jnp.fft.fft(jnp.pad(group_rows, ((0, seq_total), (0, 0))), axis=0)
        result = jnp.real(jnp.fft.ifft(filter_spec[:, None] * padded_spec, axis=0))[:seq_total]
        return result.astype(jnp.float32)

    grouped = source.reshape(seq_total, group_count, group_size).transpose(1, 0, 2)
    convolved = lax.map(one_group, (decay_rates, residues, grouped))
    convolved = convolved.transpose(1, 0, 2).reshape(seq_total, group_count * group_size)
    gated_rows = (query_feat * (convolved + skip_gain[None, :] * source)).astype(jnp.bfloat16)
    slab_width = gated_rows.shape[1] // N_TP
    summed = jnp.zeros((seq_total, out_weight.shape[1]), jnp.float32)
    for slab_index in range(N_TP):
        partial_value = jnp.dot(gated_rows[:, slab_index * slab_width:(slab_index + 1) * slab_width], out_weight[slab_index * slab_width:(slab_index + 1) * slab_width], preferred_element_type=jnp.float32)
        summed = summed + lax.optimization_barrier(partial_value.astype(jnp.bfloat16)).astype(jnp.float32)
    return summed.astype(jnp.bfloat16)
```

```python
import functools

import jax
import jax.numpy as jnp
from jax import lax
from jax.experimental import pallas as pl
from jax.experimental.pallas import tpu as pltpu
from jax.sharding import PartitionSpec as P

MESH = pl.DeviceIdType.MESH
F32 = jnp.float32
LANES = 128


def kernel(
    n_seq, n_tp, pieces,
    q_ref, k_ref, v_ref, taps_ref, rates_ref, res_ref, skip_ref, w_hbm,
    out_ref,
    w_vmem, ext_ref, qf_ref, x3_ref, y3_ref, a3_ref, ar3_ref, r3_ref, s3_ref,
    halo_out, halo_in, state_ref, gathered, carries, carry_in, gated_ref,
    acc_ref, from_left, from_right,
    w_sem, halo_sem, st_send, st_recv, ca_send, ca_recv,
    right_send, right_recv, left_send, left_recv,
):
    rows, chans = q_ref.shape
    groups, modes = rates_ref.shape
    subs = chans // LANES
    group_size = chans // groups
    owners = min(n_seq, modes)
    per_owner = modes // owners
    width = w_vmem.shape[2]
    me = lax.axis_index("seq")
    z = lax.axis_index("tp")

    loads = []
    for i in range(n_tp * pieces):
        load = pltpu.make_async_copy(
            w_hbm.at[:, pl.ds(i * width, width)], w_vmem.at[i], w_sem.at[i]
        )
        load.start()
        loads.append(load)

    barrier = pltpu.get_barrier_semaphore()
    for off in range(1, n_seq):
        pl.semaphore_signal(
            barrier, inc=1, device_id={"seq": lax.rem(me + off, n_seq)}, device_id_type=MESH
        )

    @pl.when(z > 0)
    def _():
        pl.semaphore_signal(barrier, inc=1, device_id={"tp": z - 1}, device_id_type=MESH)

    @pl.when(z < n_tp - 1)
    def _():
        pl.semaphore_signal(barrier, inc=1, device_id={"tp": z + 1}, device_id_type=MESH)

    branch_refs = (q_ref, k_ref, v_ref)
    halo_out[...] = jnp.zeros_like(halo_out)
    for b, ref in enumerate(branch_refs):
        tail = ref[rows - 16 : rows, :].astype(F32)
        halo_out[2 * b : 2 * b + 2, :] = tail[14:16]

    edges = jnp.where(z > 0, 1, 0) + jnp.where(z < n_tp - 1, 1, 0)
    pl.semaphore_wait(barrier, n_seq - 1 + edges)

    halo_copy = pltpu.make_async_remote_copy(
        src_ref=halo_out,
        dst_ref=halo_in,
        send_sem=halo_sem.at[0],
        recv_sem=halo_sem.at[1],
        device_id={"seq": lax.rem(me + 1, n_seq)},
        device_id_type=MESH,
    )

    @pl.when(me < n_seq - 1)
    def _():
        halo_copy.start()

    chan_id = lax.broadcasted_iota(jnp.int32, (groups, chans), 1)
    group_id = lax.broadcasted_iota(jnp.int32, (groups, chans), 0)
    onehot = (chan_id // group_size == group_id).astype(F32)
    dims = (((0,), (0,)), ((), ()))
    rate_nat = lax.dot_general(
        rates_ref[...], onehot, dims, precision=lax.Precision.HIGHEST, preferred_element_type=F32
    )
    res_nat = lax.dot_general(
        res_ref[...], onehot, dims, precision=lax.Precision.HIGHEST, preferred_element_type=F32
    )
    for s in range(subs):
        cols = slice(s * LANES, (s + 1) * LANES)
        rate = rate_nat[:, cols]
        a3_ref[:, s, :] = jnp.exp(-rate)
        ar3_ref[:, s, :] = jnp.exp(-rate * float(rows))
        r3_ref[:, s, :] = res_nat[:, cols]
        s3_ref[s : s + 1, :] = skip_ref[0:1, cols]

    for b, ref in enumerate(branch_refs):
        ext_ref[b, 8 : 8 + rows, :] = ref[...].astype(F32)

    @pl.when(me == 0)
    def _():
        halo_in[...] = jnp.zeros_like(halo_in)

    @pl.when(me > 0)
    def _():
        halo_copy.wait_recv()

    for b in range(3):
        ext_ref[b, 6:8, :] = halo_in[2 * b : 2 * b + 2, :]

    def feature(b, cols):
        return (
            taps_ref[0:1, cols] * ext_ref[b, 8 : 8 + rows, cols]
            + taps_ref[1:2, cols] * ext_ref[b, 7 : 7 + rows, cols]
            + taps_ref[2:3, cols] * ext_ref[b, 6 : 6 + rows, cols]
        )

    for s in range(subs):
        cols = slice(s * LANES, (s + 1) * LANES)
        x3_ref[:, s, :] = feature(1, cols) * feature(2, cols)

    decays = [a3_ref[r] for r in range(modes)]

    def state_step(t, hs):
        x = x3_ref[t]
        return tuple(decays[r] * hs[r] + x for r in range(modes))

    zero = jnp.zeros((subs, LANES), F32)
    hs = lax.fori_loop(0, rows, state_step, (zero,) * modes, unroll=4)
    for r in range(modes):
        state_ref[r] = hs[r]

    def state_copy(off):
        to = lax.rem(me + off, n_seq)
        return pltpu.make_async_remote_copy(
            src_ref=state_ref.at[pl.ds(to * per_owner, per_owner)],
            dst_ref=gathered.at[me],
            send_sem=st_send.at[off],
            recv_sem=st_recv.at[off],
            device_id={"seq": to},
            device_id_type=MESH,
        ), to

    def carry_copy(off):
        to = lax.rem(me + off, n_seq)
        return pltpu.make_async_remote_copy(
            src_ref=carries.at[to],
            dst_ref=carry_in.at[pl.ds(me * per_owner, per_owner)],
            send_sem=ca_send.at[off],
            recv_sem=ca_recv.at[off],
            device_id={"seq": to},
            device_id_type=MESH,
        ), to

    def when_owner(index, act):
        if owners == n_seq:
            act()
        else:
            pl.when(index < owners)(act)

    for off in range(1, n_seq):
        copy, to = state_copy(off)
        when_owner(to, copy.start)

    for s in range(subs):
        cols = slice(s * LANES, (s + 1) * LANES)
        qf_ref[:, cols] = feature(0, cols)

    weights = [r3_ref[r] for r in range(modes)]
    skip = s3_ref[...]

    def local_step(t, hs):
        x = x3_ref[t]
        y = skip * x
        out = []
        for r in range(modes):
            h = decays[r] * hs[r] + x
            y = y + weights[r] * h
            out.append(h)
        y3_ref[t] = y
        return tuple(out)

    lax.fori_loop(0, rows, local_step, (zero,) * modes, unroll=2)

    def own_modes():
        mine = pl.ds(me * per_owner, per_owner)
        gathered[me] = state_ref[mine]
        for off in range(1, n_seq):
            state_copy(off)[0].wait_recv()
        block_decay = ar3_ref[mine]
        carry = jnp.zeros((per_owner, subs, LANES), F32)
        for j in range(n_seq):
            carries[j] = carry
            carry = block_decay * carry + gathered[j]
        for off in range(1, n_seq):
            carry_copy(off)[0].start()
        carry_in[mine] = carries[me]

    when_owner(me, own_modes)
    for off in range(1, n_seq):
        sender = lax.rem(me - off + n_seq, n_seq)
        when_owner(sender, carry_copy(off)[0].wait_recv)

    def carry_step(t, gs):
        y = y3_ref[t]
        for r in range(modes):
            y = y + gs[r]
        y3_ref[t] = y
        return tuple(decays[r] * gs[r] for r in range(modes))

    gs = tuple(weights[r] * (decays[r] * carry_in[r]) for r in range(modes))
    lax.fori_loop(0, rows, carry_step, gs, unroll=4)

    for s in range(subs):
        cols = slice(s * LANES, (s + 1) * LANES)
        gated_ref[:, cols] = (qf_ref[:, cols] * y3_ref[:, s, :]).astype(jnp.bfloat16)

    for load in loads:
        load.wait()

    def product(i):
        return jnp.dot(gated_ref[...], w_vmem[i], preferred_element_type=F32)

    def right_copy(i):
        return pltpu.make_async_remote_copy(
            src_ref=acc_ref.at[i], dst_ref=from_left.at[i],
            send_sem=right_send.at[i], recv_sem=right_recv.at[i],
            device_id={"tp": jnp.minimum(z + 1, n_tp - 1)}, device_id_type=MESH,
        )

    def left_copy(i):
        return pltpu.make_async_remote_copy(
            src_ref=acc_ref.at[i], dst_ref=from_right.at[i],
            send_sem=left_send.at[i], recv_sem=left_recv.at[i],
            device_id={"tp": jnp.maximum(z - 1, 0)}, device_id_type=MESH,
        )

    def chain_step(step, _):
        block, piece = step // pieces, step % pieces
        right_block = n_tp - 1 - block
        left_block = block

        @pl.when(right_block > z)
        def _():
            i = right_block * pieces + piece
            part = product(i)

            @pl.when(z == 0)
            def _():
                acc_ref[i] = part.astype(jnp.bfloat16)

            @pl.when(z > 0)
            def _():
                right_copy(i).wait_recv()
                acc_ref[i] = (part + from_left[i].astype(F32)).astype(jnp.bfloat16)

            right_copy(i).start()

        @pl.when(left_block < z)
        def _():
            i = left_block * pieces + piece
            part = product(i)

            @pl.when(z == n_tp - 1)
            def _():
                acc_ref[i] = part.astype(jnp.bfloat16)

            @pl.when(z < n_tp - 1)
            def _():
                left_copy(i).wait_recv()
                acc_ref[i] = (part + from_right[i].astype(F32)).astype(jnp.bfloat16)

            left_copy(i).start()

        return 0

    lax.fori_loop(0, (n_tp - 1) * pieces, chain_step, 0)

    for piece in range(pieces):
        i = z * pieces + piece
        cols = slice(piece * width, (piece + 1) * width)
        total = product(i)
        acc_ref[i] = total.astype(jnp.bfloat16)

        @pl.when(z > 0)
        def _():
            right_copy(i).wait_recv()

        @pl.when(z < n_tp - 1)
        def _():
            left_copy(i).wait_recv()

        @pl.when(z == 0)
        def _():
            out_ref[:, cols] = (total + from_right[i].astype(F32)).astype(jnp.bfloat16)

        @pl.when(z == n_tp - 1)
        def _():
            out_ref[:, cols] = (total + from_left[i].astype(F32)).astype(jnp.bfloat16)

        @pl.when(jnp.logical_and(z > 0, z < n_tp - 1))
        def _():
            out_ref[:, cols] = (
                total + from_left[i].astype(F32) + from_right[i].astype(F32)
            ).astype(jnp.bfloat16)

    @pl.when(me < n_seq - 1)
    def _():
        halo_copy.wait_send()

    for off in range(1, n_seq):
        copy, to = state_copy(off)
        when_owner(to, copy.wait_send)
        when_owner(me, carry_copy(off)[0].wait_send)

    def drain(step, _):
        block, piece = step // pieces, step % pieces
        i = block * pieces + piece

        @pl.when(block > z)
        def _():
            right_copy(i).wait_send()

        @pl.when(block < z)
        def _():
            left_copy(i).wait_send()

        return 0

    lax.fori_loop(0, n_tp * pieces, drain, 0)


def body(n_seq, n_tp, q, k, v, taps, rates, res, skip, w):
    rows, chans = q.shape
    groups, modes = rates.shape
    subs = chans // LANES
    owners = min(n_seq, modes)
    per_owner = modes // owners
    dout = w.shape[1]
    block = dout // n_tp
    width = min(256, block)
    pieces = block // width
    total = n_tp * pieces
    vmem = pl.BlockSpec(memory_space=pltpu.VMEM)
    dma = pltpu.SemaphoreType.DMA
    return pl.pallas_call(
        functools.partial(kernel, n_seq, n_tp, pieces),
        out_shape=jax.ShapeDtypeStruct((rows, block), jnp.bfloat16),
        in_specs=[vmem] * 7 + [pl.BlockSpec(memory_space=pl.ANY)],
        out_specs=vmem,
        scratch_shapes=[
            pltpu.VMEM((total, chans, width), jnp.bfloat16),
            pltpu.VMEM((3, rows + 8, chans), F32),
            pltpu.VMEM((rows, chans), F32),
            pltpu.VMEM((rows, subs, LANES), F32),
            pltpu.VMEM((rows, subs, LANES), F32),
            pltpu.VMEM((modes, subs, LANES), F32),
            pltpu.VMEM((modes, subs, LANES), F32),
            pltpu.VMEM((modes, subs, LANES), F32),
            pltpu.VMEM((subs, LANES), F32),
            pltpu.VMEM((8, chans), F32),
            pltpu.VMEM((8, chans), F32),
            pltpu.VMEM((modes, subs, LANES), F32),
            pltpu.VMEM((n_seq, per_owner, subs, LANES), F32),
            pltpu.VMEM((n_seq, per_owner, subs, LANES), F32),
            pltpu.VMEM((modes, subs, LANES), F32),
            pltpu.VMEM((rows, chans), jnp.bfloat16),
            pltpu.VMEM((total, rows, width), jnp.bfloat16),
            pltpu.VMEM((total, rows, width), jnp.bfloat16),
            pltpu.VMEM((total, rows, width), jnp.bfloat16),
            dma((total,)),
            dma((2,)),
            dma((n_seq,)), dma((n_seq,)), dma((n_seq,)), dma((n_seq,)),
            dma((total,)), dma((total,)), dma((total,)), dma((total,)),
        ],
        compiler_params=pltpu.CompilerParams(
            collective_id=0, has_side_effects=True, vmem_limit_bytes=48 * 1024 * 1024
        ),
    )(q, k, v, taps, rates, res, skip.reshape(1, chans), w)


def solution(mesh):
    placed = (
        P("seq", "tp"),
        P("seq", "tp"),
        P("seq", "tp"),
        P(None, "tp"),
        P("tp", None),
        P("tp", None),
        P("tp"),
        P("tp", None),
    )
    return jax.shard_map(
        functools.partial(body, mesh.shape["seq"], mesh.shape["tp"]),
        mesh=mesh, in_specs=placed, out_specs=P("seq", "tp"), check_vma=False,
    )
```

```python
import functools

import jax
import jax.numpy as jnp
from jax import lax
from jax.experimental import pallas as pl
from jax.experimental.pallas import tpu as pltpu
from jax.sharding import PartitionSpec as P

MESH = pl.DeviceIdType.MESH
F32 = jnp.float32
LANES = 128


def kernel(
    n_seq, n_tp, pieces,
    q_hbm, k_hbm, v_hbm, taps_hbm, rates_hbm, res_hbm, skip_hbm, w_hbm,
    out_ref,
    qkv_ref, taps_ref, rates_ref, res_ref, skip_ref, w_vmem,
    ext_ref, qf_ref, x3_ref, y3_ref, a3_ref, ar3_ref, r3_ref, s3_ref,
    halo_out, halo_in, state_ref, gathered, carries, carry_in, gated_ref,
    acc_ref, from_mate, final_in, acc_own,
    in_sem, w_sem, halo_sem, st_send, st_recv, ca_send, ca_recv,
    out_send, mate_recv, final_recv,
):
    rows, chans = q_hbm.shape
    modes, groups = rates_ref.shape
    subs = chans // LANES
    group_size = chans // groups
    owners = min(n_seq, modes)
    per_owner = modes // owners
    width = w_vmem.shape[2]
    me = lax.axis_index("seq")
    z = lax.axis_index("tp")

    inputs = [
        pltpu.make_async_copy(src, dst, in_sem.at[i])
        for i, (src, dst) in enumerate((
            (q_hbm, qkv_ref.at[0]), (k_hbm, qkv_ref.at[1]), (v_hbm, qkv_ref.at[2]),
            (rates_hbm, rates_ref), (res_hbm, res_ref),
            (taps_hbm, taps_ref), (skip_hbm, skip_ref),
        ))
    ]
    for copy in inputs:
        copy.start()

    barrier = pltpu.get_barrier_semaphore()
    for off in range(1, n_seq):
        pl.semaphore_signal(
            barrier, inc=1, device_id={"seq": lax.rem(me + off, n_seq)}, device_id_type=MESH
        )
    for off in range(1, n_tp):
        pl.semaphore_signal(
            barrier, inc=1, device_id={"tp": lax.rem(z + off, n_tp)}, device_id_type=MESH
        )

    loads = [
        pltpu.make_async_copy(
            w_hbm.at[:, pl.ds(i * width, width)], w_vmem.at[i], w_sem.at[i]
        )
        for i in range(n_tp * pieces)
    ]

    halo_out[...] = jnp.zeros_like(halo_out)
    for b in range(3):
        inputs[b].wait()
        tail = qkv_ref[b, rows - 16 : rows, :].astype(F32)
        halo_out[2 * b : 2 * b + 2, :] = tail[14:16]
    for copy in inputs[3:]:
        copy.wait()
    for load in loads:
        load.start()

    pl.semaphore_wait(barrier, n_seq - 1 + n_tp - 1)

    halo_copy = pltpu.make_async_remote_copy(
        src_ref=halo_out,
        dst_ref=halo_in,
        send_sem=halo_sem.at[0],
        recv_sem=halo_sem.at[1],
        device_id={"seq": lax.rem(me + 1, n_seq)},
        device_id_type=MESH,
    )

    @pl.when(me < n_seq - 1)
    def _():
        halo_copy.start()

    chan_id = lax.broadcasted_iota(jnp.int32, (groups, chans), 1)
    group_id = lax.broadcasted_iota(jnp.int32, (groups, chans), 0)
    onehot = (chan_id // group_size == group_id).astype(F32)
    dims = (((1,), (0,)), ((), ()))
    rate_nat = lax.dot_general(
        rates_ref[...], onehot, dims, precision=lax.Precision.HIGHEST, preferred_element_type=F32
    )
    res_nat = lax.dot_general(
        res_ref[...], onehot, dims, precision=lax.Precision.HIGHEST, preferred_element_type=F32
    )
    for s in range(subs):
        cols = slice(s * LANES, (s + 1) * LANES)
        rate = rate_nat[:, cols]
        a3_ref[:, s, :] = jnp.exp(-rate)
        ar3_ref[:, s, :] = jnp.exp(-rate * float(rows))
        r3_ref[:, s, :] = res_nat[:, cols]
        s3_ref[s : s + 1, :] = skip_ref[0:1, cols]

    for b in range(3):
        ext_ref[b, 8 : 8 + rows, :] = qkv_ref[b].astype(F32)

    @pl.when(me == 0)
    def _():
        halo_in[...] = jnp.zeros_like(halo_in)

    @pl.when(me > 0)
    def _():
        halo_copy.wait_recv()

    for b in range(3):
        ext_ref[b, 6:8, :] = halo_in[2 * b : 2 * b + 2, :]

    def feature(b, cols):
        return (
            taps_ref[0:1, cols] * ext_ref[b, 8 : 8 + rows, cols]
            + taps_ref[1:2, cols] * ext_ref[b, 7 : 7 + rows, cols]
            + taps_ref[2:3, cols] * ext_ref[b, 6 : 6 + rows, cols]
        )

    for s in range(subs):
        cols = slice(s * LANES, (s + 1) * LANES)
        x3_ref[:, s, :] = feature(1, cols) * feature(2, cols)

    decays = [a3_ref[r] for r in range(modes)]

    def state_step(t, hs):
        x = x3_ref[t]
        return tuple(decays[r] * hs[r] + x for r in range(modes))

    zero = jnp.zeros((subs, LANES), F32)
    hs = lax.fori_loop(0, rows, state_step, (zero,) * modes, unroll=4)
    for r in range(modes):
        state_ref[r] = hs[r]

    def state_copy(off):
        to = lax.rem(me + off, n_seq)
        return pltpu.make_async_remote_copy(
            src_ref=state_ref.at[pl.ds(to * per_owner, per_owner)],
            dst_ref=gathered.at[me],
            send_sem=st_send.at[off],
            recv_sem=st_recv.at[off],
            device_id={"seq": to},
            device_id_type=MESH,
        ), to

    def carry_copy(off):
        to = lax.rem(me + off, n_seq)
        return pltpu.make_async_remote_copy(
            src_ref=carries.at[to],
            dst_ref=carry_in.at[pl.ds(me * per_owner, per_owner)],
            send_sem=ca_send.at[off],
            recv_sem=ca_recv.at[off],
            device_id={"seq": to},
            device_id_type=MESH,
        ), to

    def when_owner(index, act):
        if owners == n_seq:
            act()
        else:
            pl.when(index < owners)(act)

    for off in range(1, n_seq):
        copy, to = state_copy(off)
        when_owner(to, copy.start)

    for s in range(subs):
        cols = slice(s * LANES, (s + 1) * LANES)
        qf_ref[:, cols] = feature(0, cols)

    weights = [r3_ref[r] for r in range(modes)]
    skip = s3_ref[...]

    def local_step(t, hs):
        x = x3_ref[t]
        y = skip * x
        out = []
        for r in range(modes):
            h = decays[r] * hs[r] + x
            y = y + weights[r] * h
            out.append(h)
        y3_ref[t] = y
        return tuple(out)

    lax.fori_loop(0, rows, local_step, (zero,) * modes, unroll=2)

    def own_modes():
        mine = pl.ds(me * per_owner, per_owner)
        gathered[me] = state_ref[mine]
        for off in range(1, n_seq):
            state_copy(off)[0].wait_recv()
        block_decay = ar3_ref[mine]
        carry = jnp.zeros((per_owner, subs, LANES), F32)
        for j in range(n_seq):
            carries[j] = carry
            carry = block_decay * carry + gathered[j]
        for off in range(1, n_seq):
            carry_copy(off)[0].start()
        carry_in[mine] = carries[me]

    when_owner(me, own_modes)
    for off in range(1, n_seq):
        sender = lax.rem(me - off + n_seq, n_seq)
        when_owner(sender, carry_copy(off)[0].wait_recv)

    def carry_step(t, gs):
        y = y3_ref[t]
        for r in range(modes):
            y = y + gs[r]
        y3_ref[t] = y
        return tuple(decays[r] * gs[r] for r in range(modes))

    gs = tuple(weights[r] * (decays[r] * carry_in[r]) for r in range(modes))
    lax.fori_loop(0, rows, carry_step, gs, unroll=4)

    for s in range(subs):
        cols = slice(s * LANES, (s + 1) * LANES)
        gated_ref[:, cols] = (qf_ref[:, cols] * y3_ref[:, s, :]).astype(jnp.bfloat16)

    for load in loads:
        load.wait()

    def product(i):
        return jnp.dot(gated_ref[...], w_vmem[i], preferred_element_type=F32)

    low = lax.rem(z, 2) == 0
    pair = z // 2
    mate = z + 1 - 2 * lax.rem(z, 2)

    def mate_copy(i):
        return pltpu.make_async_remote_copy(
            src_ref=acc_ref.at[i], dst_ref=from_mate.at[i],
            send_sem=out_send.at[i], recv_sem=mate_recv.at[i],
            device_id={"tp": mate}, device_id_type=MESH,
        )

    def final_copy(block, piece, sender_pair):
        i = block * pieces + piece
        slot = sender_pair * pieces + piece
        return pltpu.make_async_remote_copy(
            src_ref=acc_ref.at[i], dst_ref=final_in.at[slot],
            send_sem=out_send.at[i], recv_sem=final_recv.at[slot],
            device_id={"tp": block}, device_id_type=MESH,
        )

    def relay_step(step, _):
        turn, piece = step // pieces, step % pieces
        block = jnp.where(low, n_tp - 1 - turn, turn)

        @pl.when(jnp.where(low, block > z + 1, block < z - 1))
        def _():
            i = block * pieces + piece
            acc_ref[i] = product(i).astype(jnp.bfloat16)
            mate_copy(i).start()

        return 0

    lax.fori_loop(0, n_tp * pieces, relay_step, 0)

    def mate_step(piece, _):
        i = mate * pieces + piece
        acc_ref[i] = product(i).astype(jnp.bfloat16)
        mate_copy(i).start()
        return 0

    lax.fori_loop(0, pieces, mate_step, 0)

    def pair_step(step, _):
        turn, piece = step // pieces, step % pieces
        block = jnp.where(low, turn, n_tp - 1 - turn)

        @pl.when(jnp.where(low, block < z, block > z))
        def _():
            i = block * pieces + piece
            part = product(i)
            mate_copy(i).wait_recv()
            acc_ref[i] = (part + from_mate[i].astype(F32)).astype(jnp.bfloat16)
            final_copy(block, piece, pair).start()

        return 0

    lax.fori_loop(0, n_tp * pieces, pair_step, 0)

    for piece in range(pieces):
        i = z * pieces + piece
        acc_own[piece] = product(i)

    for piece in range(pieces):
        i = z * pieces + piece
        cols = slice(piece * width, (piece + 1) * width)
        for off in range(1, n_tp // 2):
            sender = lax.rem(pair + off, n_tp // 2)
            final_copy(z, piece, sender).wait_recv()
            acc_own[piece] += final_in[sender * pieces + piece].astype(F32)
        mate_copy(i).wait_recv()
        out_ref[:, cols] = (acc_own[piece] + from_mate[i].astype(F32)).astype(jnp.bfloat16)

    @pl.when(me < n_seq - 1)
    def _():
        halo_copy.wait_send()

    for off in range(1, n_seq):
        copy, to = state_copy(off)
        when_owner(to, copy.wait_send)
        when_owner(me, carry_copy(off)[0].wait_send)

    def drain(step, _):
        block, piece = step // pieces, step % pieces

        @pl.when(block != z)
        def _():
            mate_copy(block * pieces + piece).wait_send()

        return 0

    lax.fori_loop(0, n_tp * pieces, drain, 0)


def body(n_seq, n_tp, q, k, v, taps, rates, res, skip, w):
    rows, chans = q.shape
    groups, modes = rates.shape
    subs = chans // LANES
    owners = min(n_seq, modes)
    per_owner = modes // owners
    dout = w.shape[1]
    block = dout // n_tp
    width = min(256, block)
    pieces = block // width
    total = n_tp * pieces
    dma = pltpu.SemaphoreType.DMA
    return pl.pallas_call(
        functools.partial(kernel, n_seq, n_tp, pieces),
        out_shape=jax.ShapeDtypeStruct((rows, block), jnp.bfloat16),
        in_specs=[pl.BlockSpec(memory_space=pltpu.HBM)] * 8,
        out_specs=pl.BlockSpec(memory_space=pltpu.VMEM),
        scratch_shapes=[
            pltpu.VMEM((3, rows, chans), jnp.bfloat16),
            pltpu.VMEM(taps.shape, F32),
            pltpu.VMEM((modes, groups), F32),
            pltpu.VMEM((modes, groups), F32),
            pltpu.VMEM((1, chans), F32),
            pltpu.VMEM((total, chans, width), jnp.bfloat16),
            pltpu.VMEM((3, rows + 8, chans), F32),
            pltpu.VMEM((rows, chans), F32),
            pltpu.VMEM((rows, subs, LANES), F32),
            pltpu.VMEM((rows, subs, LANES), F32),
            pltpu.VMEM((modes, subs, LANES), F32),
            pltpu.VMEM((modes, subs, LANES), F32),
            pltpu.VMEM((modes, subs, LANES), F32),
            pltpu.VMEM((subs, LANES), F32),
            pltpu.VMEM((8, chans), F32),
            pltpu.VMEM((8, chans), F32),
            pltpu.VMEM((modes, subs, LANES), F32),
            pltpu.VMEM((n_seq, per_owner, subs, LANES), F32),
            pltpu.VMEM((n_seq, per_owner, subs, LANES), F32),
            pltpu.VMEM((modes, subs, LANES), F32),
            pltpu.VMEM((rows, chans), jnp.bfloat16),
            pltpu.VMEM((total, rows, width), jnp.bfloat16),
            pltpu.VMEM((total, rows, width), jnp.bfloat16),
            pltpu.VMEM((n_tp // 2 * pieces, rows, width), jnp.bfloat16),
            pltpu.VMEM((pieces, rows, width), F32),
            dma((7,)),
            dma((total,)),
            dma((2,)),
            dma((n_seq,)), dma((n_seq,)), dma((n_seq,)), dma((n_seq,)),
            dma((total,)), dma((total,)), dma((n_tp // 2 * pieces,)),
        ],
        compiler_params=pltpu.CompilerParams(
            collective_id=0, has_side_effects=True, vmem_limit_bytes=63 * 1024 * 1024
        ),
    )(q, k, v, taps, rates.T, res.T, skip.reshape(1, chans), w)


def solution(mesh):
    placed = (
        P("seq", "tp"),
        P("seq", "tp"),
        P("seq", "tp"),
        P(None, "tp"),
        P("tp", None),
        P("tp", None),
        P("tp"),
        P("tp", None),
    )
    return jax.shard_map(
        functools.partial(body, mesh.shape["seq"], mesh.shape["tp"]),
        mesh=mesh, in_specs=placed, out_specs=P("seq", "tp"), check_vma=False,
    )
```

```python
import functools

import jax
import jax.numpy as jnp
from jax import lax
from jax.experimental import pallas as pl
from jax.experimental.pallas import tpu as pltpu
from jax.sharding import PartitionSpec as P

MESH = pl.DeviceIdType.MESH
F32 = jnp.float32
LANES = 128


def kernel(
    n_seq, n_tp, pieces,
    q_hbm, k_hbm, v_hbm, taps_hbm, rates_hbm, res_hbm, skip_hbm, w_hbm,
    out_ref,
    qkv_ref, taps_ref, rates_ref, res_ref, skip_ref, w_vmem,
    ext_ref, qf_ref, x3_ref, y3_ref, a3_ref, am3_ref, ar3_ref, r3_ref, s3_ref,
    halo_out, halo_in, state_ref, gathered, carries, carry_in, gated_ref,
    acc_ref, from_mate, final_in, acc_own,
    in_sem, w_sem, halo_sem, st_send, st_recv, ca_send, ca_recv,
    out_send, mate_recv, final_recv,
):
    rows, chans = q_hbm.shape
    modes, groups = rates_ref.shape
    subs = chans // LANES
    group_size = chans // groups
    owners = min(n_seq, modes)
    per_owner = modes // owners
    width = w_vmem.shape[2]
    me = lax.axis_index("seq")
    z = lax.axis_index("tp")

    inputs = [
        pltpu.make_async_copy(src, dst, in_sem.at[i])
        for i, (src, dst) in enumerate((
            (q_hbm, qkv_ref.at[0]), (k_hbm, qkv_ref.at[1]), (v_hbm, qkv_ref.at[2]),
            (rates_hbm, rates_ref), (res_hbm, res_ref),
            (taps_hbm, taps_ref), (skip_hbm, skip_ref),
        ))
    ]
    for copy in inputs:
        copy.start()

    barrier = pltpu.get_barrier_semaphore()
    for off in range(1, n_seq):
        pl.semaphore_signal(
            barrier, inc=1, device_id={"seq": lax.rem(me + off, n_seq)}, device_id_type=MESH
        )
    for off in range(1, n_tp):
        pl.semaphore_signal(
            barrier, inc=1, device_id={"tp": lax.rem(z + off, n_tp)}, device_id_type=MESH
        )

    loads = [
        pltpu.make_async_copy(
            w_hbm.at[:, pl.ds(i * width, width)], w_vmem.at[i], w_sem.at[i]
        )
        for i in range(n_tp * pieces)
    ]

    halo_out[...] = jnp.zeros_like(halo_out)
    for b in range(3):
        inputs[b].wait()
        tail = qkv_ref[b, rows - 16 : rows, :].astype(F32)
        halo_out[2 * b : 2 * b + 2, :] = tail[14:16]
    for copy in inputs[3:]:
        copy.wait()
    for load in loads:
        load.start()

    chan_id = lax.broadcasted_iota(jnp.int32, (groups, chans), 1)
    group_id = lax.broadcasted_iota(jnp.int32, (groups, chans), 0)
    onehot = (chan_id // group_size == group_id).astype(F32)
    dims = (((1,), (0,)), ((), ()))
    rate_nat = lax.dot_general(
        rates_ref[...], onehot, dims, precision=lax.Precision.HIGHEST, preferred_element_type=F32
    )
    res_nat = lax.dot_general(
        res_ref[...], onehot, dims, precision=lax.Precision.HIGHEST, preferred_element_type=F32
    )
    for s in range(subs):
        cols = slice(s * LANES, (s + 1) * LANES)
        rate = rate_nat[:, cols]
        a3_ref[:, s, :] = jnp.exp(-rate)
        am3_ref[:, s, :] = jnp.exp(-rate * float(rows - 2))
        ar3_ref[:, s, :] = jnp.exp(-rate * float(rows))
        r3_ref[:, s, :] = res_nat[:, cols]
        s3_ref[s : s + 1, :] = skip_ref[0:1, cols]

    for b in range(3):
        ext_ref[b, 0:8, :] = jnp.zeros((8, chans), F32)
        ext_ref[b, 8 : 8 + rows, :] = qkv_ref[b].astype(F32)

    pl.semaphore_wait(barrier, n_seq - 1 + n_tp - 1)

    halo_copy = pltpu.make_async_remote_copy(
        src_ref=halo_out,
        dst_ref=halo_in,
        send_sem=halo_sem.at[0],
        recv_sem=halo_sem.at[1],
        device_id={"seq": lax.rem(me + 1, n_seq)},
        device_id_type=MESH,
    )

    @pl.when(me < n_seq - 1)
    def _():
        halo_copy.start()

    def feature(b, cols, count):
        return (
            taps_ref[0:1, cols] * ext_ref[b, 8 : 8 + count, cols]
            + taps_ref[1:2, cols] * ext_ref[b, 7 : 7 + count, cols]
            + taps_ref[2:3, cols] * ext_ref[b, 6 : 6 + count, cols]
        )


    for s in range(subs):
        cols = slice(s * LANES, (s + 1) * LANES)
        x3_ref[:, s, :] = feature(1, cols, rows) * feature(2, cols, rows)

    decays = [a3_ref[r] for r in range(modes)]

    def state_step(t, hs):
        x = x3_ref[t]
        return tuple(decays[r] * hs[r] + x for r in range(modes))

    zero = jnp.zeros((subs, LANES), F32)
    hs = state_step(3, state_step(2, (zero,) * modes))
    hs = lax.fori_loop(4, rows, state_step, hs, unroll=4)
    for r in range(modes):
        state_ref[r] = hs[r]

    for s in range(subs):
        cols = slice(s * LANES, (s + 1) * LANES)
        qf_ref[:, cols] = feature(0, cols, rows)

    @pl.when(me == 0)
    def _():
        halo_in[...] = jnp.zeros_like(halo_in)

    @pl.when(me > 0)
    def _():
        halo_copy.wait_recv()

    for b in range(3):
        ext_ref[b, 6:8, :] = halo_in[2 * b : 2 * b + 2, :]

    for s in range(subs):
        cols = slice(s * LANES, (s + 1) * LANES)
        x3_ref[0:8, s, :] = feature(1, cols, 8) * feature(2, cols, 8)
        qf_ref[0:8, cols] = feature(0, cols, 8)
    first, second = x3_ref[0], x3_ref[1]
    for r in range(modes):
        state_ref[r] += am3_ref[r] * (second + a3_ref[r] * first)

    def state_copy(off):
        to = lax.rem(me + off, n_seq)
        return pltpu.make_async_remote_copy(
            src_ref=state_ref.at[pl.ds(to * per_owner, per_owner)],
            dst_ref=gathered.at[me],
            send_sem=st_send.at[off],
            recv_sem=st_recv.at[off],
            device_id={"seq": to},
            device_id_type=MESH,
        ), to

    def carry_copy(off):
        to = lax.rem(me + off, n_seq)
        return pltpu.make_async_remote_copy(
            src_ref=carries.at[to],
            dst_ref=carry_in.at[pl.ds(me * per_owner, per_owner)],
            send_sem=ca_send.at[off],
            recv_sem=ca_recv.at[off],
            device_id={"seq": to},
            device_id_type=MESH,
        ), to

    def when_owner(index, act):
        if owners == n_seq:
            act()
        else:
            pl.when(index < owners)(act)

    for off in range(1, n_seq):
        copy, to = state_copy(off)
        pl.when(jnp.logical_and(to < owners, me < n_seq - 1))(copy.start)

    weights = [r3_ref[r] for r in range(modes)]
    skip = s3_ref[...]

    def local_step(t, hs):
        x = x3_ref[t]
        y = skip * x
        out = []
        for r in range(modes):
            h = decays[r] * hs[r] + x
            y = y + weights[r] * h
            out.append(h)
        y3_ref[t] = y
        return tuple(out)

    half = rows // 2
    hs = lax.fori_loop(0, half, local_step, (zero,) * modes, unroll=2)

    def own_modes():
        mine = pl.ds(me * per_owner, per_owner)
        gathered[me] = state_ref[mine]
        for off in range(1, n_seq):
            sender = lax.rem(me - off + n_seq, n_seq)
            pl.when(sender < n_seq - 1)(state_copy(off)[0].wait_recv)
        block_decay = ar3_ref[mine]
        carry = jnp.zeros((per_owner, subs, LANES), F32)
        for j in range(n_seq):
            carries[j] = carry
            if j < n_seq - 1:
                carry = block_decay * carry + gathered[j]
        for off in range(1, n_seq):
            copy, to = carry_copy(off)
            pl.when(to > 0)(copy.start)
        carry_in[mine] = carries[me]

    when_owner(me, own_modes)
    lax.fori_loop(half, rows, local_step, hs, unroll=2)
    for off in range(1, n_seq):
        sender = lax.rem(me - off + n_seq, n_seq)
        pl.when(jnp.logical_and(sender < owners, me > 0))(carry_copy(off)[0].wait_recv)

    @pl.when(me == 0)
    def _():
        carry_in[...] = jnp.zeros_like(carry_in)

    def carry_step(t, gs):
        y = y3_ref[t]
        for r in range(modes):
            y = y + gs[r]
        y3_ref[t] = y
        return tuple(decays[r] * gs[r] for r in range(modes))

    gs = tuple(weights[r] * (decays[r] * carry_in[r]) for r in range(modes))
    lax.fori_loop(0, rows, carry_step, gs, unroll=4)

    for s in range(subs):
        cols = slice(s * LANES, (s + 1) * LANES)
        gated_ref[:, cols] = (qf_ref[:, cols] * y3_ref[:, s, :]).astype(jnp.bfloat16)

    for load in loads:
        load.wait()

    def product(i):
        return jnp.dot(gated_ref[...], w_vmem[i], preferred_element_type=F32)

    low = lax.rem(z, 2) == 0
    pair = z // 2
    mate = z + 1 - 2 * lax.rem(z, 2)

    def mate_copy(i):
        return pltpu.make_async_remote_copy(
            src_ref=acc_ref.at[i], dst_ref=from_mate.at[i],
            send_sem=out_send.at[i], recv_sem=mate_recv.at[i],
            device_id={"tp": mate}, device_id_type=MESH,
        )

    def final_copy(block, piece, sender_pair):
        i = block * pieces + piece
        slot = sender_pair * pieces + piece
        return pltpu.make_async_remote_copy(
            src_ref=acc_ref.at[i], dst_ref=final_in.at[slot],
            send_sem=out_send.at[i], recv_sem=final_recv.at[slot],
            device_id={"tp": block}, device_id_type=MESH,
        )

    def relay_step(step, _):
        turn, piece = step // pieces, step % pieces
        block = jnp.where(low, n_tp - 1 - turn, turn)

        @pl.when(jnp.where(low, block > z + 1, block < z - 1))
        def _():
            i = block * pieces + piece
            acc_ref[i] = product(i).astype(jnp.bfloat16)
            mate_copy(i).start()

        return 0

    lax.fori_loop(0, n_tp * pieces, relay_step, 0)

    def mate_step(piece, _):
        i = mate * pieces + piece
        acc_ref[i] = product(i).astype(jnp.bfloat16)
        mate_copy(i).start()
        return 0

    lax.fori_loop(0, pieces, mate_step, 0)

    def pair_step(step, _):
        turn, piece = step // pieces, step % pieces
        block = jnp.where(low, turn, n_tp - 1 - turn)

        @pl.when(jnp.where(low, block < z, block > z))
        def _():
            i = block * pieces + piece
            part = product(i)
            mate_copy(i).wait_recv()
            acc_ref[i] = (part + from_mate[i].astype(F32)).astype(jnp.bfloat16)
            final_copy(block, piece, pair).start()

        return 0

    lax.fori_loop(0, n_tp * pieces, pair_step, 0)

    for piece in range(pieces):
        i = z * pieces + piece
        acc_own[piece] = product(i)

    for piece in range(pieces):
        i = z * pieces + piece
        cols = slice(piece * width, (piece + 1) * width)
        for off in range(1, n_tp // 2):
            sender = lax.rem(pair + off, n_tp // 2)
            final_copy(z, piece, sender).wait_recv()
            acc_own[piece] += final_in[sender * pieces + piece].astype(F32)
        mate_copy(i).wait_recv()
        out_ref[:, cols] = (acc_own[piece] + from_mate[i].astype(F32)).astype(jnp.bfloat16)

    @pl.when(me < n_seq - 1)
    def _():
        halo_copy.wait_send()

    for off in range(1, n_seq):
        copy, to = state_copy(off)
        pl.when(jnp.logical_and(to < owners, me < n_seq - 1))(copy.wait_send)
        pl.when(jnp.logical_and(me < owners, to > 0))(carry_copy(off)[0].wait_send)

    def drain(step, _):
        block, piece = step // pieces, step % pieces

        @pl.when(block != z)
        def _():
            mate_copy(block * pieces + piece).wait_send()

        return 0

    lax.fori_loop(0, n_tp * pieces, drain, 0)


def body(n_seq, n_tp, q, k, v, taps, rates, res, skip, w):
    rows, chans = q.shape
    groups, modes = rates.shape
    subs = chans // LANES
    owners = min(n_seq, modes)
    per_owner = modes // owners
    dout = w.shape[1]
    block = dout // n_tp
    width = min(256, block)
    pieces = block // width
    total = n_tp * pieces
    dma = pltpu.SemaphoreType.DMA
    return pl.pallas_call(
        functools.partial(kernel, n_seq, n_tp, pieces),
        out_shape=jax.ShapeDtypeStruct((rows, block), jnp.bfloat16),
        in_specs=[pl.BlockSpec(memory_space=pltpu.HBM)] * 8,
        out_specs=pl.BlockSpec(memory_space=pltpu.VMEM),
        scratch_shapes=[
            pltpu.VMEM((3, rows, chans), jnp.bfloat16),
            pltpu.VMEM(taps.shape, F32),
            pltpu.VMEM((modes, groups), F32),
            pltpu.VMEM((modes, groups), F32),
            pltpu.VMEM((1, chans), F32),
            pltpu.VMEM((total, chans, width), jnp.bfloat16),
            pltpu.VMEM((3, rows + 8, chans), F32),
            pltpu.VMEM((rows, chans), F32),
            pltpu.VMEM((rows, subs, LANES), F32),
            pltpu.VMEM((rows, subs, LANES), F32),
            pltpu.VMEM((modes, subs, LANES), F32),
            pltpu.VMEM((modes, subs, LANES), F32),
            pltpu.VMEM((modes, subs, LANES), F32),
            pltpu.VMEM((modes, subs, LANES), F32),
            pltpu.VMEM((subs, LANES), F32),
            pltpu.VMEM((8, chans), F32),
            pltpu.VMEM((8, chans), F32),
            pltpu.VMEM((modes, subs, LANES), F32),
            pltpu.VMEM((n_seq, per_owner, subs, LANES), F32),
            pltpu.VMEM((n_seq, per_owner, subs, LANES), F32),
            pltpu.VMEM((modes, subs, LANES), F32),
            pltpu.VMEM((rows, chans), jnp.bfloat16),
            pltpu.VMEM((total, rows, width), jnp.bfloat16),
            pltpu.VMEM((total, rows, width), jnp.bfloat16),
            pltpu.VMEM((n_tp // 2 * pieces, rows, width), jnp.bfloat16),
            pltpu.VMEM((pieces, rows, width), F32),
            dma((7,)),
            dma((total,)),
            dma((2,)),
            dma((n_seq,)), dma((n_seq,)), dma((n_seq,)), dma((n_seq,)),
            dma((total,)), dma((total,)), dma((n_tp // 2 * pieces,)),
        ],
        compiler_params=pltpu.CompilerParams(
            collective_id=0, has_side_effects=True, vmem_limit_bytes=63 * 1024 * 1024
        ),
    )(q, k, v, taps, rates.T, res.T, skip.reshape(1, chans), w)


def solution(mesh):
    placed = (
        P("seq", "tp"),
        P("seq", "tp"),
        P("seq", "tp"),
        P(None, "tp"),
        P("tp", None),
        P("tp", None),
        P("tp"),
        P("tp", None),
    )
    return jax.shard_map(
        functools.partial(body, mesh.shape["seq"], mesh.shape["tp"]),
        mesh=mesh, in_specs=placed, out_specs=P("seq", "tp"), check_vma=False,
    )
```
